32 devices in a mesh: groups: 2 (over y), tensor: 16 (over z, x, core).
Axes of the slice: x: 2, y: 2, z: 4, core: 2. Of those that a mesh axis runs over, the one named last changes fastest.
Arguments:
- layer_input: bfloat16 [256, 8192], P(('groups', 'tensor')), parts along dimension 0, may hold values from -6 to 6
- out_cotangent: bfloat16 [256, 8192], P(('groups', 'tensor')), parts along dimension 0, may hold values from -6 to 6
- gate_pre: bfloat16 [256, 28672], P('groups', 'tensor'), parts along dimension 0, may hold values from -8 to 8
- up_pre: bfloat16 [256, 28672], P('groups', 'tensor'), parts along dimension 0, may hold values from -6 to 6
- down_weight: bfloat16 [28672, 8192], P('tensor'), may hold values from -0.03125 to 0.03125
- proj_in_up: bfloat16 [8192, 64], replicated, may hold values from -0.0625 to 0.0625
- proj_out_up: bfloat16 [28672, 64], P('tensor'), may hold values from -0.03125 to 0.03125
- proj_in_down: bfloat16 [28672, 64], P('tensor'), may hold values from -0.03125 to 0.03125
- proj_out_down: bfloat16 [8192, 64], replicated, may hold values from -0.0625 to 0.0625
- owner_order: int32 [32], P('groups'), parts along dimension 0, may hold values from 0 to 15, each once
- query_features: bfloat16 [64, 8192], P(('groups', 'tensor')), parts along dimension 0, may hold values from -0.0625 to 0.0625
Outputs:
- logged: bfloat16 [32, 8192], P(('groups', 'tensor')), parts along dimension 0
- scores: float32 [32, 32], P(('groups', 'tensor')), parts along dimension 0
The draws below stay inside these ranges and needn't reach their ends.
There are 2 independent parts, one for each index of `groups`. The reference program is written for one: setup_inputs(seed, part) draws one part's arguments, and reference() takes and returns one part's arrays. A program takes and returns all parts, laid end to end along the dimension named above; an argument that names none is the same for every part. Nothing has to cross between parts.
Inputs may be any that keep to these rules, and one draw needn't show every extreme that they name: `owner_order`: each example appears exactly once; logged row j is owned by device j // 1 of tensor.
All inputs are finite; a program needn't handle non-finite values.
Results may differ from the reference program's by a relative error of at most 0.0051.
Values may be sent and summed in bfloat16 or wider, within the bound.
A program may use at most 128 MiB of HBM per device.

```python
import jax
import jax.numpy as jnp
from jax import lax

D = 8192
FF = 28672
PROJ = 64
LEN = 8
EXAMPLES = 16
TOKENS = 128
QUERIES = 32


def block_scale(stream_key, dims, cuts, low, high):
    level = 1.0
    for position, parts in cuts:
        heights = jax.random.uniform(jax.random.fold_in(jax.random.fold_in(stream_key, 6), position), (parts,), jnp.float32, low / len(cuts), high / len(cuts))
        level = level * jnp.repeat(jnp.exp(heights), dims[position] // parts).reshape((-1,) + (1,) * (len(dims) - 1 - position))
    return level


def bell_draw(key, dims, scale, limit, pieces=(), dtype=jnp.bfloat16):
    drawn = scale * jax.random.normal(key, dims, jnp.float32)
    if pieces:
        drawn = drawn * block_scale(key, dims, pieces, -0.22, 0.18)
    return jnp.clip(drawn, -limit, limit).astype(dtype)


def setup_inputs(seed: int = 0, part: int = 0) -> dict:
    key_list = jax.random.split(jax.random.key(seed), 12)
    part_splits = jax.random.split(jax.random.fold_in(key_list[11], part), 12)
    return {
        "layer_input": bell_draw(part_splits[0], (TOKENS, D), 1.0, 6.0, ((0, 16),)),
        "out_cotangent": bell_draw(part_splits[1], (TOKENS, D), 1.0, 6.0, ((0, 16),)),
        "gate_pre": bell_draw(part_splits[2], (TOKENS, FF), 1.5, 8.0, ((1, 16),)),
        "up_pre": bell_draw(part_splits[3], (TOKENS, FF), 1.0, 6.0, ((1, 16),)),
        "down_weight": bell_draw(key_list[4], (FF, D), FF ** -0.5, 0.03125, ((0, 16),)),
        "proj_in_up": bell_draw(key_list[5], (D, PROJ), D ** -0.5, 0.0625),
        "proj_out_up": bell_draw(key_list[6], (FF, PROJ), FF ** -0.5, 0.03125, ((0, 16),)),
        "proj_in_down": bell_draw(key_list[7], (FF, PROJ), FF ** -0.5, 0.03125, ((0, 16),)),
        "proj_out_down": bell_draw(key_list[8], (D, PROJ), D ** -0.5, 0.0625),
        "owner_order": jax.random.permutation(part_splits[9], EXAMPLES).astype(jnp.int32),
        "query_features": bell_draw(part_splits[10], (QUERIES, 2 * PROJ * PROJ), (2 * PROJ * PROJ) ** -0.5, 0.0625, ((0, 16),)),
    }


def outer_blocks(left, right):
    left = left.reshape(-1, LEN, left.shape[1])
    right = right.reshape(-1, LEN, right.shape[1])
    prod = jnp.einsum("elk,elm->ekm", left, right, precision=lax.Precision.HIGHEST)
    return prod.reshape(prod.shape[0], -1)


def reference(layer_input, out_cotangent, gate_pre, up_pre, down_weight, proj_in_up, proj_out_up, proj_in_down, proj_out_down, owner_order, query_features):
    grad_hidden = jnp.dot(out_cotangent, down_weight.T, preferred_element_type=jnp.float32)
    gate_act = jax.nn.silu(gate_pre.astype(jnp.float32))
    hidden = (gate_act * up_pre.astype(jnp.float32)).astype(jnp.bfloat16)
    grad_up = (grad_hidden * gate_act).astype(jnp.bfloat16)
    in_up = jnp.dot(layer_input, proj_in_up, preferred_element_type=jnp.float32)
    out_up = jnp.dot(grad_up, proj_out_up, preferred_element_type=jnp.float32)
    in_down = jnp.dot(hidden, proj_in_down, preferred_element_type=jnp.float32)
    out_down = jnp.dot(out_cotangent, proj_out_down, preferred_element_type=jnp.float32)
    blocks = jnp.concatenate([outer_blocks(out_up, in_up), outer_blocks(out_down, in_down)], axis=1)
    logged = jnp.take(blocks, owner_order, axis=0).astype(jnp.bfloat16)
    scores = jnp.dot(logged, query_features.T, preferred_element_type=jnp.float32)
    return logged, scores
```

```python
import functools

import jax
import jax.numpy as jnp
from jax import lax
from jax.experimental import pallas as pl
from jax.experimental.pallas import tpu as pltpu
from jax.sharding import PartitionSpec as P

LEN = 8
OUTER = 4
CHUNKS = 4
F32, BF16 = jnp.float32, jnp.bfloat16


def kernel(
    n,
    li_ref, oc_ref, gate_ref, up_ref, w_ref, piu_ref, pou_ref, pid_ref, pod_ref, order_ref, q_ref,
    logged_ref, scores_ref,
    li, oc, q, gate, up, w, piu, pou, pid, pod,
    g, x, acc, act, mine, all_u, in_down, part, stage, got, qtmp, rows,
    loc_sem, w_sem,
    z_send, z_recv, x_send, x_recv, c_send, c_recv, u_send, u_recv, r_send, r_recv,
):
    a_n, b_n = OUTER, n // (2 * OUTER)
    chunks = w.shape[0]
    width = w.shape[2]
    half = width // 2
    feat = w.shape[1]
    tile = 256 if feat % 256 == 0 else feat
    tiles = feat // tile
    side = pou.shape[1]
    me = lax.axis_index("tensor")
    core = lax.rem(me, 2)
    b = lax.rem(me // 2, b_n)
    a = me // (2 * b_n)
    slot = (core * b_n + b) * a_n + a

    def device(a_, b_, core_):
        return {"tensor": (a_ * b_n + b_) * 2 + core_}

    small = [(oc_ref, oc), (q_ref, q), (gate_ref, gate), (up_ref, up), (pid_ref, pid),
             (li_ref, li), (piu_ref, piu), (pod_ref, pod), (pou_ref, pou)]
    local = {}
    for i, (src, dst) in enumerate(small):
        local[i] = pltpu.make_async_copy(src, dst, loc_sem.at[i])
        local[i].start()
    w_copies = []
    for c in range(chunks):
        cp = pltpu.make_async_copy(w_ref.at[:, pl.ds(c * width, width)], w.at[c], w_sem.at[c])
        cp.start()
        w_copies.append(cp)

    barrier = pltpu.get_barrier_semaphore()

    @pl.loop(1, n)
    def _(k):
        pl.semaphore_signal(barrier, inc=1, device_id={"tensor": lax.rem(me + k, n)},
                            device_id_type=pl.DeviceIdType.MESH)

    local[0].wait()
    for c in range(chunks):
        lo = oc[:, c * width:c * width + half].astype(F32)
        hi = oc[:, c * width + half:(c + 1) * width].astype(F32)
        g[c, slot] = jnp.concatenate([lo, hi], axis=0).astype(BF16)
    local[1].wait()
    qn = q.shape[0]
    qs = 16 // qn
    qw = q.shape[1] // qs
    for s in range(qs):
        qtmp[s * qn:(s + 1) * qn, :] = q[:, s * qw:(s + 1) * qw].astype(F32)
    g[chunks, slot] = qtmp[...].astype(BF16)

    pl.semaphore_wait(barrier, n - 1)

    def z_copy(c, k):
        return pltpu.make_async_remote_copy(
            src_ref=g.at[c, slot], dst_ref=g.at[c, slot],
            send_sem=z_send.at[c, k], recv_sem=z_recv.at[c, k],
            device_id=device(lax.rem(a + k, a_n), b, core), device_id_type=pl.DeviceIdType.MESH)

    def x_copy(c, k):
        column = pl.ds((core * b_n + b) * a_n, a_n)
        return pltpu.make_async_remote_copy(
            src_ref=g.at[c, column], dst_ref=g.at[c, column],
            send_sem=x_send.at[c, k], recv_sem=x_recv.at[c, k],
            device_id=device(a, lax.rem(b + k, b_n), core), device_id_type=pl.DeviceIdType.MESH)

    def c_copy(c, k):
        column = pl.ds((core * b_n + lax.rem(b - k + b_n, b_n)) * a_n, a_n)
        return pltpu.make_async_remote_copy(
            src_ref=g.at[c, column], dst_ref=g.at[c, column],
            send_sem=c_send.at[c, k], recv_sem=c_recv.at[c, k],
            device_id=device(a, b, 1 - core), device_id_type=pl.DeviceIdType.MESH)

    for c in range(chunks + 1):
        for k in range(1, a_n):
            z_copy(c, k).start()

    def forward_z(c):
        for k in range(1, a_n):
            z_copy(c, k).wait_recv()
        for k in range(1, b_n):
            x_copy(c, k).start()
        c_copy(c, 0).start()

    def forward_x(c):
        for k in range(1, b_n):
            x_copy(c, k).wait_recv()
            c_copy(c, k).start()

    def arrived(c):
        for k in range(b_n):
            c_copy(c, k).wait_recv()

    for i in (2, 3, 4):
        local[i].wait()
    for i in range(tiles):
        sl = slice(i * tile, (i + 1) * tile)
        v = gate[:, sl].astype(F32)
        ga = v / (1.0 + jnp.exp(-v))
        act[:, sl] = ga
        hidden = (ga * up[:, sl].astype(F32)).astype(BF16)
        d = jnp.dot(hidden, pid[sl, :], preferred_element_type=F32)
        if i == 0:
            in_down[...] = d
        else:
            in_down[...] += d
    for i in (5, 6, 7):
        local[i].wait()
    own_iu = jnp.dot(li[...], piu[...], preferred_element_type=F32)
    own_od = jnp.dot(oc[...], pod[...], preferred_element_type=F32)
    own_u = jnp.concatenate([own_iu, own_od], axis=1)
    mine[...] = own_u
    all_u[me] = own_u

    def u_copy(k):
        return pltpu.make_async_remote_copy(
            src_ref=mine, dst_ref=all_u.at[me], send_sem=u_send.at[0], recv_sem=u_recv.at[0],
            device_id={"tensor": lax.rem(me + k, n)}, device_id_type=pl.DeviceIdType.MESH)

    @pl.loop(1, n)
    def _(k):
        u_copy(k).start()

    def pack(c):
        @pl.loop(0, n // 2)
        def _(i):
            s0 = lax.rem(i, b_n) * a_n + i // b_n
            g0 = g[c, s0].astype(F32)
            g1 = g[c, s0 + b_n * a_n].astype(F32)
            at = pl.ds(pl.multiple_of(i * 16, 16), 16)
            x[at, 0:half] = jnp.concatenate([g0[0:8], g1[0:8]], axis=0).astype(BF16)
            x[at, half:width] = jnp.concatenate([g0[8:16], g1[8:16]], axis=0).astype(BF16)

    nt = (((1,), (1,)), ((), ()))

    def multiply(c):
        w_copies[c].wait()
        arrived(c)
        pack(c)

        @pl.loop(0, tiles)
        def _(i):
            at = pl.ds(pl.multiple_of(i * tile, tile), tile)
            d = lax.dot_general(x[...], w[c, at, :], nt, preferred_element_type=F32)
            if c == 0:
                acc[i] = d
            else:
                acc[i] += d

    forward_z(0)
    for c in range(chunks):
        forward_z(c + 1)
        forward_x(c)
        multiply(c)

    local[8].wait()
    out_up = jnp.zeros((x.shape[0], side), F32)
    for i in range(tiles):
        sl = slice(i * tile, (i + 1) * tile)
        gu = (acc[i] * act[:, sl]).astype(BF16)
        out_up += jnp.dot(gu, pou[sl, :], preferred_element_type=F32)
    part[...] = jnp.concatenate([out_up, in_down[...]], axis=1).reshape(part.shape)

    def r_copy(k):
        to = lax.rem(me + k, n)
        return pltpu.make_async_remote_copy(
            src_ref=stage.at[to], dst_ref=got.at[me], send_sem=r_send.at[0], recv_sem=r_recv.at[0],
            device_id={"tensor": to}, device_id_type=pl.DeviceIdType.MESH)

    @pl.loop(1, n)
    def _(k):
        to = lax.rem(me + k, n)
        stage[to] = part[order_ref[to]]
        r_copy(k).start()

    got[me] = part[order_ref[me]]
    forward_x(chunks)

    def total(ref, send_sem, recv_sem):
        span = ref.at[pl.ds(0, n - 1)]
        return pltpu.make_async_remote_copy(
            src_ref=span, dst_ref=span, send_sem=send_sem.at[0], recv_sem=recv_sem.at[0],
            device_id={"tensor": lax.rem(me + 1, n)}, device_id_type=pl.DeviceIdType.MESH)

    total(all_u, u_send, u_recv).wait_recv()
    total(got, r_send, r_recv).wait_recv()
    summed = jnp.sum(got[...], axis=0)
    u = all_u[order_ref[me]]
    lane = lax.broadcasted_iota(jnp.int32, (LEN, 2 * side), 1)
    first = lane < side
    left = jnp.where(first, summed, u)
    right = jnp.where(first, u, summed)
    swapped = jnp.concatenate([right[:, side:], right[:, :side]], axis=1)
    right_up = jnp.where(first, right, swapped)
    right_down = jnp.where(first, swapped, right)
    per = qw // (2 * side)
    for p in range(side):
        rgt = right_up if p < side // 2 else right_down
        lft = jnp.where(first, left[:, 2 * p:2 * p + 1], left[:, 2 * p + 1:2 * p + 2])
        rows[p // per:p // per + 1, (p % per) * 2 * side:(p % per + 1) * 2 * side] = jnp.sum(
            lft * rgt, axis=0, keepdims=True)
    for s in range(qs):
        logged_ref[:, s * qw:(s + 1) * qw] = rows[s:s + 1, :].astype(BF16)

    arrived(chunks)
    gq = g[chunks].reshape(n * 16, qw)
    prod = lax.dot_general(rows[...].astype(BF16), gq, nt, preferred_element_type=F32)
    r_i = lax.broadcasted_iota(jnp.int32, (qs, n * 16), 1)
    s_i = lax.broadcasted_iota(jnp.int32, (qs, n * 16), 0)
    prod = jnp.where(lax.rem(r_i, 16) // qn == s_i, prod, 0.0)
    r_j = lax.broadcasted_iota(jnp.int32, (n * 16, n * qn), 0)
    c_j = lax.broadcasted_iota(jnp.int32, (n * 16, n * qn), 1)
    sl_j = r_j // 16
    dev_j = (lax.rem(sl_j, a_n) * b_n + lax.rem(sl_j // a_n, b_n)) * 2 + sl_j // (a_n * b_n)
    pick = jnp.where(dev_j * qn + lax.rem(r_j, qn) == c_j, 1.0, 0.0).astype(F32)
    sc = jnp.dot(prod, pick, preferred_element_type=F32, precision=lax.Precision.HIGHEST)
    scores_ref[...] = jnp.sum(sc, axis=0, keepdims=True)

    for c in range(chunks + 1):
        for k in range(1, a_n):
            z_copy(c, k).wait_send()
        for k in range(1, b_n):
            x_copy(c, k).wait_send()
        for k in range(b_n):
            c_copy(c, k).wait_send()
    total(all_u, u_send, u_recv).wait_send()
    total(got, r_send, r_recv).wait_send()


def shards(n, li, oc, gate, up, w, piu, pou, pid, pod, order, q):
    tokens, feat = gate.shape
    model = w.shape[1]
    side = piu.shape[1]
    width = model // CHUNKS
    tile = 256 if feat % 256 == 0 else feat
    b_n = n // (2 * OUTER)
    vm = pltpu.VMEM
    dma = pltpu.SemaphoreType.DMA
    anywhere = pl.BlockSpec(memory_space=pl.ANY)
    qn = q.shape[0]
    return pl.pallas_call(
        functools.partial(kernel, n),
        out_shape=(jax.ShapeDtypeStruct((1, q.shape[1]), BF16),
                   jax.ShapeDtypeStruct((1, n * qn), F32)),
        in_specs=[anywhere] * 9 + [pl.BlockSpec(memory_space=pltpu.SMEM), anywhere],
        out_specs=(pl.BlockSpec(memory_space=pltpu.VMEM),) * 2,
        scratch_shapes=[
            vm(li.shape, BF16), vm(oc.shape, BF16), vm(q.shape, BF16),
            vm(gate.shape, BF16), vm(up.shape, BF16), vm((CHUNKS, feat, width), BF16),
            vm(piu.shape, BF16), vm(pou.shape, BF16), vm(pid.shape, BF16), vm(pod.shape, BF16),
            vm((CHUNKS + 1, n, 16, width // 2), BF16),
            vm((tokens, width), BF16),
            vm((feat // tile, tokens, tile), F32),
            vm((tokens, feat), F32),
            vm((LEN, 2 * side), F32), vm((n, LEN, 2 * side), F32),
            vm((tokens, side), F32),
            vm((n, LEN, 2 * side), F32), vm((n, LEN, 2 * side), F32), vm((n, LEN, 2 * side), F32),
            vm((16, q.shape[1] * qn // 16), F32), vm((16 // qn, q.shape[1] * qn // 16), F32),
            dma((9,)), dma((CHUNKS,)),
            dma((CHUNKS + 1, OUTER)), dma((CHUNKS + 1, OUTER)),
            dma((CHUNKS + 1, b_n)), dma((CHUNKS + 1, b_n)),
            dma((CHUNKS + 1, b_n)), dma((CHUNKS + 1, b_n)),
            dma((1,)), dma((1,)), dma((1,)), dma((1,)),
        ],
        compiler_params=pltpu.CompilerParams(
            collective_id=0, has_side_effects=True, vmem_limit_bytes=60 * 1024 * 1024),
        cost_estimate=pl.CostEstimate(
            flops=2 * tokens * feat * model, bytes_accessed=2 * feat * model, transcendentals=tokens * feat),
    )(li, oc, gate, up, w, piu, pou, pid, pod, order, q)


def solution(mesh):
    rows = P(("groups", "tensor"), None)
    split = P("tensor", None)
    return jax.shard_map(
        functools.partial(shards, mesh.shape["tensor"]),
        mesh=mesh,
        in_specs=(rows, rows, P("groups", "tensor"), P("groups", "tensor"), split, P(), split, split, P(),
                  P("groups"), rows),
        out_specs=(rows, rows),
        check_vma=False,
    )
```

```python
import functools

import jax
import jax.numpy as jnp
from jax import lax
from jax.experimental import pallas as pl
from jax.experimental.pallas import tpu as pltpu
from jax.sharding import PartitionSpec as P

LEN = 8
OUTER = 4
CHUNKS = 4
F32, BF16 = jnp.float32, jnp.bfloat16


def kernel(
    n,
    li_ref, oc_ref, gate_ref, up_ref, w_ref, piu_ref, pou_ref, pid_ref, pod_ref, order_ref, q_ref,
    logged_ref, scores_ref,
    li, oc, q, gate, up, w, piu, pou, pid, pod,
    g, x, acc, act, mine, all_u, in_down, part, stage, got, qtmp, rows,
    loc_sem, w_sem,
    z_send, z_recv, x_send, x_recv, c_send, c_recv, u_send, u_recv, r_send, r_recv,
):
    a_n, b_n = OUTER, n // (2 * OUTER)
    chunks = w.shape[0]
    width = w.shape[2]
    half = width // 2
    feat = w.shape[1]
    tile = 896 if feat % 896 == 0 else feat
    tiles = feat // tile
    side = pou.shape[0]
    nt = (((1,), (1,)), ((), ()))
    me = lax.axis_index("tensor")
    core = lax.rem(me, 2)
    b = lax.rem(me // 2, b_n)
    a = me // (2 * b_n)
    slot = (core * b_n + b) * a_n + a

    def device(a_, b_, core_):
        return {"tensor": (a_ * b_n + b_) * 2 + core_}

    small = [(oc_ref, oc), (q_ref, q), (gate_ref, gate), (up_ref, up), (pid_ref, pid),
             (li_ref, li), (piu_ref, piu), (pod_ref, pod), (pou_ref, pou)]
    local = {}
    for i, (src, dst) in enumerate(small):
        local[i] = pltpu.make_async_copy(src, dst, loc_sem.at[i])
        local[i].start()
    w_copies = []
    for c in range(chunks):
        cp = pltpu.make_async_copy(w_ref.at[:, pl.ds(c * width, width)], w.at[c], w_sem.at[c])
        cp.start()
        w_copies.append(cp)

    barrier = pltpu.get_barrier_semaphore()

    near = [device(lax.rem(a + k, a_n), b, core) for k in range(1, a_n)]
    near += [device(a, lax.rem(b + k, b_n), core) for k in range(1, b_n)] + [device(a, b, 1 - core)]
    for peer in near:
        pl.semaphore_signal(barrier, inc=1, device_id=peer, device_id_type=pl.DeviceIdType.MESH)

    local[0].wait()
    for c in range(chunks):
        lo = oc[:, c * width:c * width + half].astype(F32)
        hi = oc[:, c * width + half:(c + 1) * width].astype(F32)
        g[c, slot] = jnp.concatenate([lo, hi], axis=0).astype(BF16)
    local[1].wait()
    qn = q.shape[0]
    qs = 16 // qn
    qw = q.shape[1] // qs
    for s in range(qs):
        qtmp[s * qn:(s + 1) * qn, :] = q[:, s * qw:(s + 1) * qw].astype(F32)
    g[chunks, slot] = qtmp[...].astype(BF16)

    pl.semaphore_wait(barrier, len(near))

    base = (core * b_n + b) * a_n

    def z_copy(c, s, to, relay=False):
        return pltpu.make_async_remote_copy(
            src_ref=g.at[c, base + s], dst_ref=g.at[c, base + s],
            send_sem=z_send.at[c, a_n if relay else to], recv_sem=z_recv.at[c, s],
            device_id=device(to, b, core), device_id_type=pl.DeviceIdType.MESH)

    def x_copy(c, k, s):
        return pltpu.make_async_remote_copy(
            src_ref=g.at[c, base + s], dst_ref=g.at[c, base + s],
            send_sem=x_send.at[c, k, s], recv_sem=x_recv.at[c, k, s],
            device_id=device(a, lax.rem(b + k, b_n), core), device_id_type=pl.DeviceIdType.MESH)

    def c_copy(c, k):
        column = pl.ds((core * b_n + lax.rem(b - k + b_n, b_n)) * a_n, a_n)
        return pltpu.make_async_remote_copy(
            src_ref=g.at[c, column], dst_ref=g.at[c, column],
            send_sem=c_send.at[c, k], recv_sem=c_recv.at[c, k],
            device_id=device(a, b, 1 - core), device_id_type=pl.DeviceIdType.MESH)

    steps = (1, -1, 2, -2)

    def reach(step):
        return (a + step >= 0) & (a + step < a_n)

    def start(c):
        for step in steps:
            @pl.when(reach(step))
            def _():
                z_copy(c, a, a + step).start()
        for k in range(1, b_n):
            x_copy(c, k, a).start()

    def relays(c, op):
        for s, via, to in ((0, 2, 3), (3, 1, 0)):
            @pl.when(a == via)
            def _():
                op(z_copy(c, s, to, True))

    for c in range(chunks + 1):
        start(c)

    def forward_z(c):
        for step in (1, -1, 2, -2, 3, -3):
            @pl.when(reach(step))
            def _():
                s = a + step
                z_copy(c, s, a).wait_recv()
                for k in range(1, b_n):
                    x_copy(c, k, s).start()
            if step in (2, -2):
                @pl.when(a == (1 if step == 2 else 2))
                def _():
                    z_copy(c, a + step, 0 if step == 2 else 3, True).start()
        c_copy(c, 0).start()

    def forward_x(c):
        for k in range(1, b_n):
            for s in range(a_n):
                x_copy(c, k, s).wait_recv()
            c_copy(c, k).start()

    def arrived(c):
        for k in range(b_n):
            c_copy(c, k).wait_recv()

    for i in (2, 3, 4):
        local[i].wait()
    for i in range(tiles):
        sl = slice(i * tile, (i + 1) * tile)
        v = gate[:, sl].astype(F32)
        ga = v / (1.0 + jnp.exp(-v))
        act[:, sl] = ga
        hidden = (ga * up[:, sl].astype(F32)).astype(BF16)
        d = lax.dot_general(hidden, pid[:, sl], nt, preferred_element_type=F32)
        if i == 0:
            in_down[...] = d
        else:
            in_down[...] += d
    for i in (5, 6, 7):
        local[i].wait()
    own_iu = lax.dot_general(li[...], piu[...], nt, preferred_element_type=F32)
    own_od = lax.dot_general(oc[...], pod[...], nt, preferred_element_type=F32)
    own_u = jnp.concatenate([own_iu, own_od], axis=1)
    mine[...] = own_u
    all_u[me] = own_u

    def u_copy(k):
        return pltpu.make_async_remote_copy(
            src_ref=mine, dst_ref=all_u.at[me], send_sem=u_send.at[0], recv_sem=u_recv.at[0],
            device_id={"tensor": lax.rem(me + k, n)}, device_id_type=pl.DeviceIdType.MESH)

    def send_u():
        @pl.loop(1, n)
        def _(k):
            u_copy(k).start()

    def pack(c):
        @pl.loop(0, n // 2)
        def _(i):
            s0 = lax.rem(i, b_n) * a_n + i // b_n
            g0 = g[c, s0].astype(F32)
            g1 = g[c, s0 + b_n * a_n].astype(F32)
            at = pl.ds(pl.multiple_of(i * 16, 16), 16)
            x[at, 0:half] = jnp.concatenate([g0[0:8], g1[0:8]], axis=0).astype(BF16)
            x[at, half:width] = jnp.concatenate([g0[8:16], g1[8:16]], axis=0).astype(BF16)

    def multiply(c):
        w_copies[c].wait()
        arrived(c)
        pack(c)

        @pl.loop(0, tiles)
        def _(i):
            at = pl.ds(pl.multiple_of(i * tile, tile), tile)
            d = lax.dot_general(x[...], w[c, at, :], nt, preferred_element_type=F32)
            if c == 0:
                acc[i] = d
            else:
                acc[i] += d

    forward_z(0)
    for c in range(chunks):
        forward_z(c + 1)
        forward_x(c)
        if c > 0:
            multiply(c - 1)
        if c == 1:
            send_u()
    multiply(chunks - 1)

    local[8].wait()
    out_up = jnp.zeros((x.shape[0], side), F32)
    for i in range(tiles):
        sl = slice(i * tile, (i + 1) * tile)
        gu = (acc[i] * act[:, sl]).astype(BF16)
        out_up += lax.dot_general(gu, pou[:, sl], nt, preferred_element_type=F32)
    part[...] = jnp.concatenate([out_up, in_down[...]], axis=1).reshape(part.shape)

    def r_copy(k):
        to = lax.rem(me + k, n)
        return pltpu.make_async_remote_copy(
            src_ref=stage.at[to], dst_ref=got.at[me], send_sem=r_send.at[0], recv_sem=r_recv.at[0],
            device_id={"tensor": to}, device_id_type=pl.DeviceIdType.MESH)

    @pl.loop(1, n)
    def _(k):
        to = lax.rem(me + k, n)
        stage[to] = part[order_ref[to]]
        r_copy(k).start()

    got[me] = part[order_ref[me]]
    forward_x(chunks)

    def total(ref, send_sem, recv_sem):
        span = ref.at[pl.ds(0, n - 1)]
        return pltpu.make_async_remote_copy(
            src_ref=span, dst_ref=span, send_sem=send_sem.at[0], recv_sem=recv_sem.at[0],
            device_id={"tensor": lax.rem(me + 1, n)}, device_id_type=pl.DeviceIdType.MESH)

    total(all_u, u_send, u_recv).wait_recv()
    total(got, r_send, r_recv).wait_recv()
    summed = jnp.sum(got[...], axis=0)
    u = all_u[order_ref[me]]
    lane = lax.broadcasted_iota(jnp.int32, (LEN, 2 * side), 1)
    first = lane < side
    left = jnp.where(first, summed, u)
    right = jnp.where(first, u, summed)
    swapped = jnp.concatenate([right[:, side:], right[:, :side]], axis=1)
    right_up = jnp.where(first, right, swapped)
    right_down = jnp.where(first, swapped, right)
    per = qw // (2 * side)
    for p in range(side):
        rgt = right_up if p < side // 2 else right_down
        lft = jnp.where(first, left[:, 2 * p:2 * p + 1], left[:, 2 * p + 1:2 * p + 2])
        rows[p // per:p // per + 1, (p % per) * 2 * side:(p % per + 1) * 2 * side] = jnp.sum(
            lft * rgt, axis=0, keepdims=True)
    for s in range(qs):
        logged_ref[:, s * qw:(s + 1) * qw] = rows[s:s + 1, :].astype(BF16)

    arrived(chunks)
    gq = g[chunks].reshape(n * 16, qw)
    prod = lax.dot_general(rows[...].astype(BF16), gq, nt, preferred_element_type=F32)
    r_i = lax.broadcasted_iota(jnp.int32, (qs, n * 16), 1)
    s_i = lax.broadcasted_iota(jnp.int32, (qs, n * 16), 0)
    prod = jnp.where(lax.rem(r_i, 16) // qn == s_i, prod, 0.0)
    r_j = lax.broadcasted_iota(jnp.int32, (n * 16, n * qn), 0)
    c_j = lax.broadcasted_iota(jnp.int32, (n * 16, n * qn), 1)
    sl_j = r_j // 16
    dev_j = (lax.rem(sl_j, a_n) * b_n + lax.rem(sl_j // a_n, b_n)) * 2 + sl_j // (a_n * b_n)
    pick = jnp.where(dev_j * qn + lax.rem(r_j, qn) == c_j, 1.0, 0.0).astype(F32)
    sc = jnp.dot(prod, pick, preferred_element_type=F32, precision=lax.Precision.HIGHEST)
    scores_ref[...] = jnp.sum(sc, axis=0, keepdims=True)

    for c in range(chunks + 1):
        for step in steps:
            @pl.when(reach(step))
            def _():
                z_copy(c, a, a + step).wait_send()
        relays(c, lambda copy: copy.wait_send())
        for k in range(1, b_n):
            for s in range(a_n):
                x_copy(c, k, s).wait_send()
        for k in range(b_n):
            c_copy(c, k).wait_send()
    total(all_u, u_send, u_recv).wait_send()
    total(got, r_send, r_recv).wait_send()


def shards(n, li, oc, gate, up, w, piu, pou, pid, pod, order, q):
    tokens, feat = gate.shape
    model = w.shape[1]
    side = piu.shape[1]
    piu, pou, pid, pod = piu.T, pou.T, pid.T, pod.T
    width = model // CHUNKS
    tile = 896 if feat % 896 == 0 else feat
    b_n = n // (2 * OUTER)
    vm = pltpu.VMEM
    dma = pltpu.SemaphoreType.DMA
    anywhere = pl.BlockSpec(memory_space=pl.ANY)
    qn = q.shape[0]
    return pl.pallas_call(
        functools.partial(kernel, n),
        out_shape=(jax.ShapeDtypeStruct((1, q.shape[1]), BF16),
                   jax.ShapeDtypeStruct((1, n * qn), F32)),
        in_specs=[anywhere] * 9 + [pl.BlockSpec(memory_space=pltpu.SMEM), anywhere],
        out_specs=(pl.BlockSpec(memory_space=pltpu.VMEM),) * 2,
        scratch_shapes=[
            vm(li.shape, BF16), vm(oc.shape, BF16), vm(q.shape, BF16),
            vm(gate.shape, BF16), vm(up.shape, BF16), vm((CHUNKS, feat, width), BF16),
            vm(piu.shape, BF16), vm(pou.shape, BF16), vm(pid.shape, BF16), vm(pod.shape, BF16),
            vm((CHUNKS + 1, n, 16, width // 2), BF16),
            vm((tokens, width), BF16),
            vm((feat // tile, tokens, tile), F32),
            vm((tokens, feat), F32),
            vm((LEN, 2 * side), F32), vm((n, LEN, 2 * side), F32),
            vm((tokens, side), F32),
            vm((n, LEN, 2 * side), F32), vm((n, LEN, 2 * side), F32), vm((n, LEN, 2 * side), F32),
            vm((16, q.shape[1] * qn // 16), F32), vm((16 // qn, q.shape[1] * qn // 16), F32),
            dma((9,)), dma((CHUNKS,)),
            dma((CHUNKS + 1, OUTER + 1)), dma((CHUNKS + 1, OUTER)),
            dma((CHUNKS + 1, b_n, OUTER)), dma((CHUNKS + 1, b_n, OUTER)),
            dma((CHUNKS + 1, b_n)), dma((CHUNKS + 1, b_n)),
            dma((1,)), dma((1,)), dma((1,)), dma((1,)),
        ],
        compiler_params=pltpu.CompilerParams(
            collective_id=0, has_side_effects=True, vmem_limit_bytes=60 * 1024 * 1024),
        cost_estimate=pl.CostEstimate(
            flops=2 * tokens * feat * model, bytes_accessed=2 * feat * model, transcendentals=tokens * feat),
    )(li, oc, gate, up, w, piu, pou, pid, pod, order, q)


def solution(mesh):
    rows = P(("groups", "tensor"), None)
    split = P("tensor", None)
    return jax.shard_map(
        functools.partial(shards, mesh.shape["tensor"]),
        mesh=mesh,
        in_specs=(rows, rows, P("groups", "tensor"), P("groups", "tensor"), split, P(), split, split, P(),
                  P("groups"), rows),
        out_specs=(rows, rows),
        check_vma=False,
    )
```
